32 devices in a mesh: groups: 2 (over y), expert: 4 (over z), sub: 4 (over x, core).
Axes of the slice: x: 2, y: 2, z: 4, core: 2. Of those that a mesh axis runs over, the one named last changes fastest.
Arguments:
- tokens: bfloat16 [512, 7168], P(('groups', 'expert', 'sub')), parts along dimension 0, may hold values from -6 to 6
- route_ids: int32 [512, 2], P(('groups', 'expert', 'sub')), parts along dimension 0, may hold values from 0 to 3, all different within a row; in each aligned block of 16 rows (0 to 15, 16 to 31, ...) at most 12 rows name the same one
- weight_index: int32 [512, 2], P(('groups', 'expert', 'sub')), parts along dimension 0, may hold values from 0 to 63
- combine_table: float32 [64], replicated, may hold values from 0.05 to 1
- w_gate: bfloat16 [4, 7168, 1024], P('expert', None, 'sub'), may hold values from -0.0625 to 0.0625
- w_up: bfloat16 [4, 7168, 1024], P('expert', None, 'sub'), may hold values from -0.0625 to 0.0625
- w_down: bfloat16 [4, 1024, 7168], P('expert', 'sub'), may hold values from -0.1875 to 0.1875
Outputs:
- mixed: bfloat16 [512, 7168], P(('groups', 'expert', 'sub')), parts along dimension 0
The draws below stay inside these ranges and needn't reach their ends.
There are 2 independent parts, one for each index of `groups`. The reference program is written for one: setup_inputs(seed, part) draws one part's arguments, and reference() takes and returns one part's arrays. A program takes and returns all parts, laid end to end along the dimension named above; an argument that names none is the same for every part. Nothing has to cross between parts.
Inputs may be any that keep to these rules, and one draw needn't show every extreme that they name: `route_ids`: each row names 2 different experts; among the 16 rows of one device no expert is named by more than 12 of them, a bound that some block reaches.
All inputs are finite; a program needn't handle non-finite values.
Results may differ from the reference program's by a relative error of at most 0.013.
Values may be sent and summed in bfloat16 or wider, within the bound.
A program may use at most 128 MiB of HBM per device.

```python
import math
import jax
import jax.numpy as jnp
import numpy as np
from jax import lax

D = 7168
FF = 1024
TOK_DEV = 16
TABLE = 64
EXPERTS = 4
TOPK = 2
CAP = 12
ROWS = 256
N_EXPERT = 4
N_SUB = 4


def set_ends(entries, own_key, least, top_value):
    index_at = [jax.random.randint(jax.random.fold_in(own_key, axis), (), 0, length) for axis, length in enumerate(entries.shape)]
    widest = entries.shape.index(max(entries.shape))
    beside = index_at[:widest] + [(index_at[widest] + 1) % entries.shape[widest]] + index_at[widest + 1:]
    return entries.at[tuple(index_at)].set(least).at[tuple(beside)].set(top_value)


def block_levels(own_key, extent, shards, low, largest):
    loudness = 1.0
    for position, shards_of in shards:
        heights = jax.random.uniform(jax.random.fold_in(jax.random.fold_in(own_key, 6), position), (shards_of,), jnp.float32, low / len(shards), largest / len(shards))
        loudness = loudness * jnp.repeat(jnp.exp(heights), extent[position] // shards_of).reshape((-1,) + (1,) * (len(extent) - 1 - position))
    return loudness


def deal_out(own_key, own, number, rows, number_of, top, bound, skew):
    order = jax.random.permutation(own_key, number_of)
    heavy_load, common = shares(number_of, rows * top, bound, skew, True), shares(number_of, rows * top, bound, skew, False)
    places = jnp.arange(number_of)

    def named(tallies, offset_by):
        used = int((tallies > 0).sum())
        fixed = max(1, used // 4)
        moved = fixed + (places - fixed + offset_by * (used - fixed)) % max(1, number_of - fixed)
        return jnp.zeros((number_of,), jnp.int32).at[order[jnp.where(places < fixed, places, moved)]].set(jnp.asarray(tallies, jnp.int32))

    tallies = jnp.where(number % 4 == 0, named(heavy_load, number // 4), named(common, number - number // 4 - 1))
    mixed = jax.random.permutation(jax.random.fold_in(own, 3), number_of)
    source_of, sink = mixed[0:number_of // 2 * 2:2], mixed[1:number_of // 2 * 2:2]
    room = jnp.minimum(tallies[source_of] - 1, bound - tallies[sink]) // 2
    room = jnp.where((source_of == order[0]) | (sink == order[0]) | (tallies[sink] == 0), 0, jnp.maximum(room, 0))
    moved = jax.random.randint(jax.random.fold_in(own, 4), (number_of // 2,), 0, 1 << 20) % (room + 1)
    tallies = tallies.at[source_of].add(-moved).at[sink].add(moved)
    items = jnp.searchsorted(jnp.cumsum(tallies), jnp.arange(rows * top), side="right").astype(jnp.int32)
    listing = items.reshape(top, rows).T
    listing = listing[jax.random.permutation(jax.random.fold_in(own, 1), rows)]
    offset_by = jax.random.randint(jax.random.fold_in(own, 2), (rows, 1), 0, top)
    return jnp.take_along_axis(listing, (jnp.arange(top)[None, :] + offset_by) % top, axis=1)


def shares(number_of, total, most, slope, full):
    loads = [(1 << 20) // math.isqrt(rank ** slope) + 1 for rank in range(1, number_of + 1)]
    largest = most if full else min(most, max(-(-total // number_of), total * loads[0] // sum(loads)))
    least = 1 if total - largest >= number_of - 1 else 0
    holding, rest = [largest] + [least] * (number_of - 1), total - largest - least * (number_of - 1)
    while rest > 0:
        movable = [i for i in range(1, number_of) if holding[i] < largest] or [i for i in range(1, number_of) if holding[i] < most]
        mass, budget = sum([loads[i] for i in movable]), rest
        for i in movable:
            extra = min(most - holding[i], max(1, budget * loads[i] // mass), rest)
            holding[i] = holding[i] + extra
            rest = rest - extra
    return np.array(holding)


def noise(own_key, dims, width, limit, cuts=(), kind=jnp.bfloat16):
    entries = jax.random.normal(own_key, dims, jnp.float32) * width
    if len(cuts) > 0:
        entries = block_levels(own_key, dims, cuts, -0.22, 0.18) * entries
    return jnp.clip(entries, min=-limit, max=limit).astype(kind)


def setup_inputs(seed: int = 0, part: int = 0) -> dict:
    key_list = jax.random.split(jax.random.key(seed), 8)
    own_keys = jax.random.split(jax.random.fold_in(key_list[7], part), 8)
    tokens = noise(own_keys[0], (ROWS, D), 1.0, 6.0, ((0, 16),))
    route_ids_keys = jax.random.split(jax.random.fold_in(own_keys[1], 1), ROWS // TOK_DEV)
    route_ids_turns = jax.random.permutation(jax.random.fold_in(own_keys[1], 3), ROWS // TOK_DEV)
    route_ids = jax.vmap(lambda own, number: deal_out(jax.random.fold_in(own_keys[1], 2), own, number, TOK_DEV, EXPERTS, TOPK, CAP, 2))(route_ids_keys, route_ids_turns).reshape((ROWS, TOPK))
    weight_index = set_ends(jax.random.randint(own_keys[2], (ROWS, TOPK), 0, TABLE), jax.random.fold_in(own_keys[2], 1), 0, TABLE - 1).astype(jnp.int32)
    combine_table = jnp.clip(jnp.exp(jax.random.uniform(key_list[3], (TABLE,), jnp.float32, math.log(0.05), math.log(1.0))), 0.05, 1.0)
    w_gate = noise(key_list[4], (EXPERTS, D, FF), D ** -0.5, 0.0625, ((0, 4), (2, 4)))
    w_up = noise(key_list[5], (EXPERTS, D, FF), D ** -0.5, 0.0625, ((0, 4), (2, 4)))
    w_down = noise(key_list[6], (EXPERTS, FF, D), FF ** -0.5, 0.1875, ((0, 4), (1, 4)))
    return {"tokens": tokens, "route_ids": route_ids, "weight_index": weight_index, "combine_table": combine_table, "w_gate": w_gate, "w_up": w_up, "w_down": w_down}


def reference(tokens, route_ids, weight_index, combine_table, w_gate, w_up, w_down):
    n_rows, n_width = tokens.shape
    devices_all = N_EXPERT * N_SUB
    slice_width = FF // N_SUB
    picks = route_ids.reshape(devices_all, TOK_DEV * TOPK)
    onehot = (picks[:, :, None] == jnp.arange(EXPERTS, dtype=jnp.int32)[None, None, :]).astype(jnp.int32)
    earlier = jnp.cumsum(onehot, axis=1) - onehot
    slot = jnp.sum(earlier * onehot, axis=2).astype(jnp.int32)
    source = jnp.broadcast_to(jnp.arange(devices_all, dtype=jnp.int32)[:, None], picks.shape)
    row_ids = (source * TOK_DEV + jnp.arange(TOK_DEV * TOPK, dtype=jnp.int32)[None, :] // TOPK).astype(jnp.int32)
    lookup = jnp.full((EXPERTS, devices_all, CAP), n_rows, jnp.int32).at[picks, source, slot].set(row_ids)
    padded = jnp.concatenate([tokens, jnp.zeros((1, n_width), jnp.bfloat16)], axis=0)

    def serve(expert_id):
        chosen = padded[lookup[expert_id].reshape(-1)].astype(jnp.float32)
        gate = jnp.dot(chosen, w_gate[expert_id].astype(jnp.float32), precision=lax.Precision.HIGHEST)
        upper = jnp.dot(chosen, w_up[expert_id].astype(jnp.float32), precision=lax.Precision.HIGHEST)
        hidden = (jax.nn.silu(gate) * upper).astype(jnp.bfloat16)
        pieces = jnp.einsum("nsf,sfd->nsd", hidden.astype(jnp.float32).reshape(-1, N_SUB, slice_width),
                            w_down[expert_id].astype(jnp.float32).reshape(N_SUB, slice_width, n_width),
                            precision=lax.Precision.HIGHEST)
        return jnp.sum(pieces.astype(jnp.bfloat16).astype(jnp.float32), axis=1).astype(jnp.bfloat16)

    outputs = lax.map(serve, jnp.arange(EXPERTS, dtype=jnp.int32))
    picked = outputs[picks, source * CAP + slot].reshape(n_rows, TOPK, n_width)
    weights = combine_table[weight_index]
    total = jnp.einsum("rk,rkd->rd", weights, picked.astype(jnp.float32), precision=lax.Precision.HIGHEST)
    return (2.5 * total / jnp.sum(weights, axis=1)[:, None]).astype(jnp.bfloat16)
```

```python
import functools

import jax
import jax.numpy as jnp
from jax import lax
from jax.experimental import pallas as pl
from jax.experimental.pallas import tpu as pltpu
from jax.sharding import PartitionSpec as P

MESH = pl.DeviceIdType.MESH
EXTRA = 128
HALF = 64


def order_of(place, n, step):
    both = jnp.minimum(place, n - 1 - place)
    far = (step + 1) // 2
    near = jnp.where(step % 2 == 1, place - far, place + far)
    rest = jnp.where(place < n - 1 - place, step, n - 1 - step)
    return jnp.where(step <= 2 * both, near, rest)


def coefficients(ids, index, table, n_expert):
    rows, topk = ids.shape
    lane = lax.broadcasted_iota(jnp.int32, (rows, EXTRA), 1)
    entry = lax.broadcasted_iota(jnp.int32, (rows, table.shape[1]), 1)
    named = jnp.zeros((rows, EXTRA), jnp.float32)
    total = jnp.zeros((rows, 1), jnp.float32)
    for k in range(topk):
        weight = jnp.sum(jnp.where(entry == index[:, k : k + 1], table, 0.0), axis=1, keepdims=True)
        named += jnp.where(lane % HALF == ids[:, k : k + 1], weight, 0.0)
        total += weight
    factor = 2.5 * named / total
    high = factor.astype(jnp.bfloat16)
    low = (factor - high.astype(jnp.float32)).astype(jnp.bfloat16)
    return jnp.where(lane < HALF, high.astype(jnp.float32), low.astype(jnp.float32)).astype(jnp.bfloat16)


def kernel(
    n, tok_ref, ids_ref, index_ref, table_ref, wg_hbm, wu_hbm, wd_hbm, out_ref,
    rows_buf, wg, wu, wd, part, core_in, x_out, x_in, z_out, z_right, z_left,
    w_sem, tok_sem,
    zr_send, zl_send, z_recv, xa_send, xa_recv, ca_send, ca_recv, cb_send, cb_recv,
    c_send, c_recv, x_send, x_recv, r_send, r_recv, l_send, l_recv,
):
    me = lax.axis_index("expert")
    sub = lax.axis_index("sub")
    cross, core = sub // 2, sub % 2
    other_core = {"sub": cross * 2 + 1 - core}
    other_x = {"sub": (1 - cross) * 2 + core}
    width = tok_ref.shape[1]
    nr = tok_ref.shape[0]

    copies_w = [
        pltpu.make_async_copy(wg_hbm.at[0], wg, w_sem.at[0]),
        pltpu.make_async_copy(wu_hbm.at[0], wu, w_sem.at[1]),
        pltpu.make_async_copy(wd_hbm.at[0], wd, w_sem.at[2]),
    ]

    def place(c, x):
        return pl.ds(pl.multiple_of((c * 2 + x) * nr, nr), nr)

    mine = place(core, cross)
    copy_tok = pltpu.make_async_copy(tok_ref, rows_buf.at[me, mine, pl.ds(0, width)], tok_sem)
    copy_tok.start()

    barrier = pltpu.get_barrier_semaphore()
    pl.semaphore_signal(barrier, inc=1, device_id=other_core, device_id_type=MESH)
    pl.semaphore_signal(barrier, inc=1, device_id=other_x, device_id_type=MESH)

    @pl.when(me > 0)
    def _():
        pl.semaphore_signal(barrier, inc=1, device_id={"expert": me - 1}, device_id_type=MESH)

    @pl.when(me < n - 1)
    def _():
        pl.semaphore_signal(barrier, inc=1, device_id={"expert": me + 1}, device_id_type=MESH)

    rows_buf[me, mine, pl.ds(width, EXTRA)] = coefficients(
        ids_ref[...], index_ref[...], table_ref[...], n
    )
    peers = 2 + jnp.where(me > 0, 1, 0) + jnp.where(me < n - 1, 1, 0)
    pl.semaphore_wait(barrier, peers)
    copy_tok.wait()

    def remote(src, dst, send, recv, device):
        return pltpu.make_async_remote_copy(
            src_ref=src, dst_ref=dst, send_sem=send, recv_sem=recv,
            device_id=device, device_id_type=MESH,
        )

    def to_right(b):
        ref = rows_buf.at[b, mine]
        return remote(ref, ref, zr_send.at[b], z_recv.at[b], {"expert": me + 1})

    def to_left(b):
        ref = rows_buf.at[b, mine]
        return remote(ref, ref, zl_send.at[b], z_recv.at[b], {"expert": me - 1})

    def across(b):
        ref = rows_buf.at[b, mine]
        return remote(ref, ref, xa_send.at[b], xa_recv.at[b], other_x)

    def beside(b):
        ref = rows_buf.at[b, mine]
        return remote(ref, ref, ca_send.at[b], ca_recv.at[b], other_core)

    def beside_far(b):
        ref = rows_buf.at[b, place(core, 1 - cross)]
        return remote(ref, ref, cb_send.at[b], cb_recv.at[b], other_core)

    def part_beside(b):
        return remote(
            part.at[b, pl.ds(pl.multiple_of((1 - core) * 2 * nr, nr), 2 * nr)],
            core_in.at[b], c_send.at[b], c_recv.at[b], other_core,
        )

    def part_across(b):
        return remote(x_out.at[b], x_in.at[b], x_send.at[b], x_recv.at[b], other_x)

    def part_right(b):
        return remote(z_out.at[b], z_right.at[b], r_send.at[b], r_recv.at[b], {"expert": me + 1})

    def part_left(b):
        return remote(z_out.at[b], z_left.at[b], l_send.at[b], l_recv.at[b], {"expert": me - 1})

    def spread(b):
        @pl.when((b <= me) & (me < n - 1))
        def _():
            to_right(b).start()

        @pl.when((b >= me) & (me > 0))
        def _():
            to_left(b).start()

        across(b).start()
        beside(b).start()

    spread(me)
    for copy in copies_w:
        copy.start()
    for copy in copies_w:
        copy.wait()

    depth = 1024

    def compute(b):
        gate = jnp.zeros((4 * nr, wg.shape[1]), jnp.float32)
        upper = jnp.zeros((4 * nr, wg.shape[1]), jnp.float32)
        for k in range(0, width, depth):
            piece = rows_buf[b, :, k : k + depth]
            gate += jnp.dot(piece, wg[k : k + depth, :], preferred_element_type=jnp.float32)
            upper += jnp.dot(piece, wu[k : k + depth, :], preferred_element_type=jnp.float32)
        extra = rows_buf[b, :, width : width + EXTRA].astype(jnp.float32)
        lane = lax.broadcasted_iota(jnp.int32, extra.shape, 1)
        factor = jnp.sum(jnp.where(lane % HALF == me, extra, 0.0), axis=1, keepdims=True)
        hidden = (gate / (1.0 + jnp.exp(-gate)) * upper * factor).astype(jnp.bfloat16)
        for k in range(0, width, depth):
            part[b, :, k : k + depth] = jnp.dot(
                hidden, wd[:, k : k + depth], preferred_element_type=jnp.float32
            ).astype(jnp.bfloat16)

    def gather_step(k, carry):
        @pl.when(k < n)
        def _():
            b = order_of(me, n, k)
            to_right(b).wait_recv()
            spread(b)

        b = order_of(me, n, k - 1)
        across(b).wait_recv()
        beside_far(b).start()
        beside(b).wait_recv()
        beside_far(b).wait_recv()
        compute(b)
        part_beside(b).start()
        return carry

    lax.fori_loop(1, n + 1, gather_step, 0)

    far_rows = pl.ds(pl.multiple_of((1 - cross) * nr, nr), nr)
    own_rows = pl.ds(pl.multiple_of(cross * nr, nr), nr)

    def cross_step(k, carry):
        b = order_of(me, n, n - 1 - k)
        part_beside(b).wait_recv()
        x_out[b] = (
            part[b, place(core, 1 - cross)].astype(jnp.float32)
            + core_in[b, far_rows].astype(jnp.float32)
        ).astype(jnp.bfloat16)
        part_across(b).start()
        return carry

    lax.fori_loop(0, n, cross_step, 0)

    def reduced(b):
        return (
            part[b, mine].astype(jnp.float32)
            + core_in[b, own_rows].astype(jnp.float32)
            + x_in[b].astype(jnp.float32)
        )

    def return_step(k, carry):
        b = order_of(me, n, n - 1 - k)
        part_across(b).wait_recv()

        @pl.when(b > me)
        def _():
            @pl.when(me > 0)
            def _():
                part_right(b).wait_recv()
                z_out[b] = (reduced(b) + z_right[b].astype(jnp.float32)).astype(jnp.bfloat16)

            @pl.when(me == 0)
            def _():
                z_out[b] = reduced(b).astype(jnp.bfloat16)

            part_right(b).start()

        @pl.when(b < me)
        def _():
            @pl.when(me < n - 1)
            def _():
                part_left(b).wait_recv()
                z_out[b] = (reduced(b) + z_left[b].astype(jnp.float32)).astype(jnp.bfloat16)

            @pl.when(me == n - 1)
            def _():
                z_out[b] = reduced(b).astype(jnp.bfloat16)

            part_left(b).start()

        return carry

    lax.fori_loop(0, n - 1, return_step, 0)

    part_across(me).wait_recv()

    @pl.when(me > 0)
    def _():
        part_right(me).wait_recv()

    @pl.when(me < n - 1)
    def _():
        part_left(me).wait_recv()

    @pl.when(me == 0)
    def _():
        out_ref[...] = (reduced(me) + z_left[me].astype(jnp.float32)).astype(jnp.bfloat16)

    @pl.when(me == n - 1)
    def _():
        out_ref[...] = (reduced(me) + z_right[me].astype(jnp.float32)).astype(jnp.bfloat16)

    @pl.when((me > 0) & (me < n - 1))
    def _():
        out_ref[...] = (
            reduced(me) + z_left[me].astype(jnp.float32) + z_right[me].astype(jnp.float32)
        ).astype(jnp.bfloat16)

    def finish(b, carry):
        @pl.when((b <= me) & (me < n - 1))
        def _():
            to_right(b).wait_send()

        @pl.when((b >= me) & (me > 0))
        def _():
            to_left(b).wait_send()

        across(b).wait_send()
        beside(b).wait_send()
        beside_far(b).wait_send()
        part_beside(b).wait_send()
        part_across(b).wait_send()

        @pl.when(b > me)
        def _():
            part_right(b).wait_send()

        @pl.when(b < me)
        def _():
            part_left(b).wait_send()

        return carry

    lax.fori_loop(0, n, finish, 0)


def fused(tokens, route_ids, weight_index, combine_table, w_gate, w_up, w_down):
    n = lax.axis_size("expert")
    rows, width = tokens.shape
    units = w_gate.shape[2]
    group = 4 * rows
    bf16 = jnp.bfloat16
    vmem = pl.BlockSpec(memory_space=pltpu.VMEM)
    hbm = pl.BlockSpec(memory_space=pl.ANY)
    dma = pltpu.SemaphoreType.DMA
    block = pltpu.VMEM((n, rows, width), bf16)
    return pl.pallas_call(
        functools.partial(kernel, n),
        out_shape=jax.ShapeDtypeStruct((rows, width), bf16),
        in_specs=[hbm, vmem, vmem, vmem, hbm, hbm, hbm],
        out_specs=vmem,
        scratch_shapes=[
            pltpu.VMEM((n, group, width + EXTRA), bf16),
            pltpu.VMEM((width, units), bf16),
            pltpu.VMEM((width, units), bf16),
            pltpu.VMEM((units, width), bf16),
            pltpu.VMEM((n, group, width), bf16),
            pltpu.VMEM((n, 2 * rows, width), bf16),
            block, block, block, block, block,
            dma((3,)), dma,
        ] + [dma((n,))] * 17,
        compiler_params=pltpu.CompilerParams(
            collective_id=0, has_side_effects=True, vmem_limit_bytes=56 * 2**20
        ),
    )(tokens, route_ids, weight_index, combine_table[None, :], w_gate, w_up, w_down)


def fits(tokens, w_gate):
    n, subs = lax.axis_size("expert"), lax.axis_size("sub")
    rows, width = tokens.shape
    held = n * rows * 15 + 3 * w_gate.shape[2]
    return (
        subs == 4 and 1 < n <= HALF and rows % 16 == 0 and width % 1024 == 0
        and held * width * 2 <= 44 * 2**20
    )


def expert_partial(rows_in, w_gate, w_up, w_down):
    gate = jnp.dot(rows_in, w_gate[0], preferred_element_type=jnp.float32)
    upper = jnp.dot(rows_in, w_up[0], preferred_element_type=jnp.float32)
    hidden = (jax.nn.silu(gate) * upper).astype(jnp.bfloat16)
    return jnp.dot(hidden, w_down[0], preferred_element_type=jnp.float32)


def shards(tokens, route_ids, weight_index, combine_table, w_gate, w_up, w_down):
    if fits(tokens, w_gate):
        return fused(tokens, route_ids, weight_index, combine_table, w_gate, w_up, w_down)
    n_expert = lax.axis_size("expert")
    n_rows, n_width = tokens.shape
    topk = route_ids.shape[1]
    capacity = max(n_rows * topk * 3 // (2 * n_expert), n_rows * topk // n_expert + 2)
    slots_all = n_expert * capacity
    flat_ids = route_ids.reshape(-1)
    onehot = (flat_ids[:, None] == jnp.arange(n_expert, dtype=jnp.int32)[None, :]).astype(jnp.int32)
    earlier = jnp.cumsum(onehot, axis=0) - onehot
    slot = jnp.sum(earlier * onehot, axis=1)
    target = (flat_ids * capacity + slot).reshape(n_rows, topk)
    positions = jnp.arange(slots_all, dtype=jnp.int32)
    select = jnp.any(target[None, :, :] == positions[:, None, None], axis=2)
    send_rows = jnp.dot(
        select.astype(jnp.bfloat16), tokens, preferred_element_type=jnp.float32
    ).astype(jnp.bfloat16)
    landed = lax.all_to_all(send_rows, "expert", split_axis=0, concat_axis=0, tiled=True)
    gathered = lax.all_gather(landed, "sub", axis=0, tiled=True)
    summed = lax.psum_scatter(
        expert_partial(gathered, w_gate, w_up, w_down).astype(jnp.bfloat16),
        "sub",
        scatter_dimension=0,
        tiled=True,
    )
    returned = lax.all_to_all(summed, "expert", split_axis=0, concat_axis=0, tiled=True)
    table_size = combine_table.shape[0]
    weights = jnp.sum(
        jnp.where(
            weight_index[:, :, None] == jnp.arange(table_size, dtype=jnp.int32)[None, None, :],
            combine_table[None, None, :],
            0.0,
        ),
        axis=2,
    )
    mixing = jnp.sum(
        jnp.where(target[:, :, None] == positions[None, None, :], weights[:, :, None], 0.0), axis=1
    )
    total = jnp.dot(mixing, returned.astype(jnp.float32), precision=lax.Precision.HIGHEST)
    return (2.5 * total / jnp.sum(weights, axis=1)[:, None]).astype(jnp.bfloat16)


def solution(mesh):
    return jax.shard_map(
        shards,
        mesh=mesh,
        in_specs=(
            P(("groups", "expert", "sub"), None),
            P(("groups", "expert", "sub"), None),
            P(("groups", "expert", "sub"), None),
            P(),
            P("expert", None, "sub"),
            P("expert", None, "sub"),
            P("expert", "sub", None),
        ),
        out_specs=P(("groups", "expert", "sub"), None),
        check_vma=False,
    )
```

```python
import functools

import jax
import jax.numpy as jnp
from jax import lax
from jax.experimental import pallas as pl
from jax.experimental.pallas import tpu as pltpu
from jax.sharding import PartitionSpec as P

MESH = pl.DeviceIdType.MESH
EXTRA = 128
HALF = 64
CUTS = 2
AHEAD = 2


def order_of(place, n, step):
    both = jnp.minimum(place, n - 1 - place)
    far = (step + 1) // 2
    left = place < n - 1 - place
    near = jnp.where((step % 2 == 1) == left, place - far, place + far)
    rest = jnp.where(left, step, n - 1 - step)
    return jnp.where(step <= 2 * both, near, rest)


def column(row):
    size = row.shape[1]
    spot = lax.broadcasted_iota(jnp.int32, (size, size), 0)
    same = spot == lax.broadcasted_iota(jnp.int32, (size, size), 1)
    picked = jnp.where(same, row.astype(jnp.float32), 0.0)
    return jnp.sum(picked, axis=1, keepdims=True).astype(jnp.int32)


def coefficients(ids, index, table):
    topk, rows = ids.shape
    lane = lax.broadcasted_iota(jnp.int32, (rows, EXTRA), 1)
    entry = lax.broadcasted_iota(jnp.int32, (rows, table.shape[1]), 1)
    named = jnp.zeros((rows, EXTRA), jnp.float32)
    total = jnp.zeros((rows, 1), jnp.float32)
    for k in range(topk):
        weight = jnp.sum(jnp.where(entry == column(index[k : k + 1, :]), table, 0.0), axis=1, keepdims=True)
        named += jnp.where(lane % HALF == column(ids[k : k + 1, :]), weight, 0.0)
        total += weight
    factor = 2.5 * named / total
    high = factor.astype(jnp.bfloat16)
    low = (factor - high.astype(jnp.float32)).astype(jnp.bfloat16)
    return jnp.where(lane < HALF, high.astype(jnp.float32), low.astype(jnp.float32)).astype(jnp.bfloat16)


def kernel(
    n, tok_ref, ids_ref, index_ref, table_ref, wg_hbm, wu_hbm, wd_hbm, out_ref,
    rows_buf, wg, wu, wd, part, core_in, x_out, x_in, z_out, z_right, z_left,
    w_sem, tok_sem,
    zr_send, zl_send, z_recv, xa_send, xa_recv, ca_send, ca_recv, cb_send, cb_recv,
    c_send, c_recv, x_send, x_recv, r_send, r_recv, l_send, l_recv,
):
    me = lax.axis_index("expert")
    sub = lax.axis_index("sub")
    cross, core = sub // 2, sub % 2
    other_core = {"sub": cross * 2 + 1 - core}
    other_x = {"sub": (1 - cross) * 2 + core}
    width = tok_ref.shape[1]
    nr = tok_ref.shape[0]

    copies_w = [
        pltpu.make_async_copy(wg_hbm.at[0], wg, w_sem.at[0]),
        pltpu.make_async_copy(wu_hbm.at[0], wu, w_sem.at[1]),
        pltpu.make_async_copy(wd_hbm.at[0], wd, w_sem.at[2]),
    ]

    def place(c, x):
        return pl.ds(pl.multiple_of((c * 2 + x) * nr, nr), nr)

    mine = place(core, cross)
    copy_tok = pltpu.make_async_copy(tok_ref, rows_buf.at[me, mine, pl.ds(0, width)], tok_sem)
    copy_tok.start()
    for copy in copies_w:
        copy.start()

    barrier = pltpu.get_barrier_semaphore()
    pl.semaphore_signal(barrier, inc=1, device_id=other_core, device_id_type=MESH)
    pl.semaphore_signal(barrier, inc=1, device_id=other_x, device_id_type=MESH)

    @pl.when(me > 0)
    def _():
        pl.semaphore_signal(barrier, inc=1, device_id={"expert": me - 1}, device_id_type=MESH)

    @pl.when(me < n - 1)
    def _():
        pl.semaphore_signal(barrier, inc=1, device_id={"expert": me + 1}, device_id_type=MESH)

    rows_buf[me, mine, pl.ds(width, EXTRA)] = coefficients(
        ids_ref[...], index_ref[...], table_ref[...]
    )
    peers = 2 + jnp.where(me > 0, 1, 0) + jnp.where(me < n - 1, 1, 0)
    pl.semaphore_wait(barrier, peers)
    copy_tok.wait()

    def remote(src, dst, send, recv, device):
        return pltpu.make_async_remote_copy(
            src_ref=src, dst_ref=dst, send_sem=send, recv_sem=recv,
            device_id=device, device_id_type=MESH,
        )

    half = width // CUTS

    def cols(h):
        return pl.ds(h * half, half + (EXTRA if h == CUTS - 1 else 0))

    def cut(h):
        return pl.ds(h * half, half)

    def to_right(b, h):
        ref = rows_buf.at[b, mine, cols(h)]
        return remote(ref, ref, zr_send.at[b, h], z_recv.at[b, h], {"expert": me + 1})

    def to_left(b, h):
        ref = rows_buf.at[b, mine, cols(h)]
        return remote(ref, ref, zl_send.at[b, h], z_recv.at[b, h], {"expert": me - 1})

    def across(b, h):
        ref = rows_buf.at[b, mine, cols(h)]
        return remote(ref, ref, xa_send.at[b, h], xa_recv.at[b, h], other_x)

    def beside(b, h):
        ref = rows_buf.at[b, mine, cols(h)]
        return remote(ref, ref, ca_send.at[b, h], ca_recv.at[b, h], other_core)

    def beside_far(b, h):
        ref = rows_buf.at[b, place(core, 1 - cross), cols(h)]
        return remote(ref, ref, cb_send.at[b, h], cb_recv.at[b, h], other_core)

    def part_beside(b, h):
        return remote(
            part.at[b, pl.ds(pl.multiple_of((1 - core) * 2 * nr, nr), 2 * nr), cut(h)],
            core_in.at[b, :, cut(h)], c_send.at[b, h], c_recv.at[b, h], other_core,
        )

    def part_across(b, h):
        return remote(x_out.at[b, :, cut(h)], x_in.at[b, :, cut(h)], x_send.at[b, h], x_recv.at[b, h], other_x)

    def part_right(b, h):
        return remote(z_out.at[b, :, cut(h)], z_right.at[b, :, cut(h)], r_send.at[b, h], r_recv.at[b, h], {"expert": me + 1})

    def part_left(b, h):
        return remote(z_out.at[b, :, cut(h)], z_left.at[b, :, cut(h)], l_send.at[b, h], l_recv.at[b, h], {"expert": me - 1})

    def spread(b, h):
        @pl.when((b <= me) & (me < n - 1))
        def _():
            to_right(b, h).start()

        @pl.when((b >= me) & (me > 0))
        def _():
            to_left(b, h).start()

        across(b, h).start()
        beside(b, h).start()

    for h in range(CUTS):
        spread(me, h)
    depth = 1024

    def compute(b):
        gate = jnp.zeros((4 * nr, wg.shape[1]), jnp.float32)
        upper = jnp.zeros((4 * nr, wg.shape[1]), jnp.float32)
        for k in range(0, width, depth):
            piece = rows_buf[b, :, k : k + depth]
            gate += jnp.dot(piece, wg[k : k + depth, :], preferred_element_type=jnp.float32)
            upper += jnp.dot(piece, wu[k : k + depth, :], preferred_element_type=jnp.float32)
        extra = rows_buf[b, :, width : width + EXTRA].astype(jnp.float32)
        lane = lax.broadcasted_iota(jnp.int32, extra.shape, 1)
        factor = jnp.sum(jnp.where(lane % HALF == me, extra, 0.0), axis=1, keepdims=True)
        hidden = (gate / (1.0 + jnp.exp(-gate)) * upper * factor).astype(jnp.bfloat16)
        step = half // 4
        for h in range(CUTS):
            for k in range(h * half, (h + 1) * half, step):
                part[b, :, k : k + step] = jnp.dot(
                    hidden, wd[:, k : k + step], preferred_element_type=jnp.float32
                ).astype(jnp.bfloat16)
            part_beside(b, h).start()

    far_rows = pl.ds(pl.multiple_of((1 - cross) * nr, nr), nr)
    own_rows = pl.ds(pl.multiple_of(cross * nr, nr), nr)

    def give_across(b, h):
        part_beside(b, h).wait_recv()
        x_out[b, :, cut(h)] = (
            part[b, place(core, 1 - cross), cut(h)].astype(jnp.float32)
            + core_in[b, far_rows, cut(h)].astype(jnp.float32)
        ).astype(jnp.bfloat16)
        part_across(b, h).start()

    def gather_step(k, carry):
        @pl.when(k < n)
        def _():
            b = order_of(me, n, k)
            for h in range(CUTS):
                to_right(b, h).wait_recv()
                spread(b, h)

        b = order_of(me, n, k - 1)
        for h in range(CUTS):
            across(b, h).wait_recv()
            beside_far(b, h).start()

        @pl.when(k == 1)
        def _():
            for copy in copies_w:
                copy.wait()

        @pl.when(k == n)
        def _():
            for h in range(CUTS):
                give_across(order_of(me, n, n - 2), h)

        for h in range(CUTS):
            beside(b, h).wait_recv()
            beside_far(b, h).wait_recv()
        compute(b)
        return carry

    lax.fori_loop(1, n + 1, gather_step, 0)

    back = [order_of(me, n, n - 1 - k) for k in range(n)]
    waiting = [(back[k], h) for k in range(n) if k != 1 for h in range(CUTS)]

    def next_across():
        if waiting:
            give_across(*waiting.pop(0))

    for _ in range(AHEAD):
        next_across()

    def reduced(b, h):
        return (
            part[b, mine, cut(h)].astype(jnp.float32)
            + core_in[b, own_rows, cut(h)].astype(jnp.float32)
            + x_in[b, :, cut(h)].astype(jnp.float32)
        )

    for k in (1, 0, *range(2, n - 1)):
        b = back[k]
        for h in range(CUTS):
            part_across(b, h).wait_recv()
            if k != 1:
                next_across()

            @pl.when(b > me)
            def _():
                @pl.when(me > 0)
                def _():
                    part_right(b, h).wait_recv()
                    z_out[b, :, cut(h)] = (
                        reduced(b, h) + z_right[b, :, cut(h)].astype(jnp.float32)
                    ).astype(jnp.bfloat16)

                @pl.when(me == 0)
                def _():
                    z_out[b, :, cut(h)] = reduced(b, h).astype(jnp.bfloat16)

                part_right(b, h).start()

            @pl.when(b < me)
            def _():
                @pl.when(me < n - 1)
                def _():
                    part_left(b, h).wait_recv()
                    z_out[b, :, cut(h)] = (
                        reduced(b, h) + z_left[b, :, cut(h)].astype(jnp.float32)
                    ).astype(jnp.bfloat16)

                @pl.when(me == n - 1)
                def _():
                    z_out[b, :, cut(h)] = reduced(b, h).astype(jnp.bfloat16)

                part_left(b, h).start()

    for h in range(CUTS):
        part_across(me, h).wait_recv()

        @pl.when(me == 0)
        def _():
            part_left(me, h).wait_recv()
            out_ref[:, cut(h)] = (
                reduced(me, h) + z_left[me, :, cut(h)].astype(jnp.float32)
            ).astype(jnp.bfloat16)

        @pl.when(me == n - 1)
        def _():
            part_right(me, h).wait_recv()
            out_ref[:, cut(h)] = (
                reduced(me, h) + z_right[me, :, cut(h)].astype(jnp.float32)
            ).astype(jnp.bfloat16)

        @pl.when((me > 0) & (me < n - 1))
        def _():
            part_right(me, h).wait_recv()
            part_left(me, h).wait_recv()
            out_ref[:, cut(h)] = (
                reduced(me, h)
                + z_left[me, :, cut(h)].astype(jnp.float32)
                + z_right[me, :, cut(h)].astype(jnp.float32)
            ).astype(jnp.bfloat16)

    def finish(b, carry):
        for h in range(CUTS):
            @pl.when((b <= me) & (me < n - 1))
            def _():
                to_right(b, h).wait_send()

            @pl.when((b >= me) & (me > 0))
            def _():
                to_left(b, h).wait_send()

            across(b, h).wait_send()
            beside(b, h).wait_send()
            beside_far(b, h).wait_send()
            part_beside(b, h).wait_send()
            part_across(b, h).wait_send()

            @pl.when(b > me)
            def _():
                part_right(b, h).wait_send()

            @pl.when(b < me)
            def _():
                part_left(b, h).wait_send()

        return carry

    lax.fori_loop(0, n, finish, 0)


def fused(tokens, route_ids, weight_index, combine_table, w_gate, w_up, w_down):
    n = lax.axis_size("expert")
    rows, width = tokens.shape
    units = w_gate.shape[2]
    group = 4 * rows
    bf16 = jnp.bfloat16
    vmem = pl.BlockSpec(memory_space=pltpu.VMEM)
    hbm = pl.BlockSpec(memory_space=pl.ANY)
    dma = pltpu.SemaphoreType.DMA
    block = pltpu.VMEM((n, rows, width), bf16)
    return pl.pallas_call(
        functools.partial(kernel, n),
        out_shape=jax.ShapeDtypeStruct((rows, width), bf16),
        in_specs=[hbm, vmem, vmem, vmem, hbm, hbm, hbm],
        out_specs=vmem,
        scratch_shapes=[
            pltpu.VMEM((n, group, width + EXTRA), bf16),
            pltpu.VMEM((width, units), bf16),
            pltpu.VMEM((width, units), bf16),
            pltpu.VMEM((units, width), bf16),
            pltpu.VMEM((n, group, width), bf16),
            pltpu.VMEM((n, 2 * rows, width), bf16),
            block, block, block, block, block,
            dma((3,)), dma,
        ] + [dma((n, CUTS))] * 17,
        compiler_params=pltpu.CompilerParams(
            collective_id=0, has_side_effects=True, vmem_limit_bytes=56 * 2**20
        ),
    )(tokens, route_ids.T, weight_index.T, combine_table[None, :], w_gate, w_up, w_down)


def fits(tokens, w_gate):
    n, subs = lax.axis_size("expert"), lax.axis_size("sub")
    rows, width = tokens.shape
    held = n * rows * 15 + 3 * w_gate.shape[2]
    return (
        subs == 4 and n == 4 and rows % 16 == 0 and width % 1024 == 0
        and held * width * 2 <= 44 * 2**20
    )


def expert_partial(rows_in, w_gate, w_up, w_down):
    gate = jnp.dot(rows_in, w_gate[0], preferred_element_type=jnp.float32)
    upper = jnp.dot(rows_in, w_up[0], preferred_element_type=jnp.float32)
    hidden = (jax.nn.silu(gate) * upper).astype(jnp.bfloat16)
    return jnp.dot(hidden, w_down[0], preferred_element_type=jnp.float32)


def shards(tokens, route_ids, weight_index, combine_table, w_gate, w_up, w_down):
    if fits(tokens, w_gate):
        return fused(tokens, route_ids, weight_index, combine_table, w_gate, w_up, w_down)
    n_expert = lax.axis_size("expert")
    n_rows, n_width = tokens.shape
    topk = route_ids.shape[1]
    capacity = max(n_rows * topk * 3 // (2 * n_expert), n_rows * topk // n_expert + 2)
    slots_all = n_expert * capacity
    flat_ids = route_ids.reshape(-1)
    onehot = (flat_ids[:, None] == jnp.arange(n_expert, dtype=jnp.int32)[None, :]).astype(jnp.int32)
    earlier = jnp.cumsum(onehot, axis=0) - onehot
    slot = jnp.sum(earlier * onehot, axis=1)
    target = (flat_ids * capacity + slot).reshape(n_rows, topk)
    positions = jnp.arange(slots_all, dtype=jnp.int32)
    select = jnp.any(target[None, :, :] == positions[:, None, None], axis=2)
    send_rows = jnp.dot(
        select.astype(jnp.bfloat16), tokens, preferred_element_type=jnp.float32
    ).astype(jnp.bfloat16)
    landed = lax.all_to_all(send_rows, "expert", split_axis=0, concat_axis=0, tiled=True)
    gathered = lax.all_gather(landed, "sub", axis=0, tiled=True)
    summed = lax.psum_scatter(
        expert_partial(gathered, w_gate, w_up, w_down).astype(jnp.bfloat16),
        "sub",
        scatter_dimension=0,
        tiled=True,
    )
    returned = lax.all_to_all(summed, "expert", split_axis=0, concat_axis=0, tiled=True)
    table_size = combine_table.shape[0]
    weights = jnp.sum(
        jnp.where(
            weight_index[:, :, None] == jnp.arange(table_size, dtype=jnp.int32)[None, None, :],
            combine_table[None, None, :],
            0.0,
        ),
        axis=2,
    )
    mixing = jnp.sum(
        jnp.where(target[:, :, None] == positions[None, None, :], weights[:, :, None], 0.0), axis=1
    )
    total = jnp.dot(mixing, returned.astype(jnp.float32), precision=lax.Precision.HIGHEST)
    return (2.5 * total / jnp.sum(weights, axis=1)[:, None]).astype(jnp.bfloat16)


def solution(mesh):
    return jax.shard_map(
        shards,
        mesh=mesh,
        in_specs=(
            P(("groups", "expert", "sub"), None),
            P(("groups", "expert", "sub"), None),
            P(("groups", "expert", "sub"), None),
            P(),
            P("expert", None, "sub"),
            P("expert", None, "sub"),
            P("expert", "sub", None),
        ),
        out_specs=P(("groups", "expert", "sub"), None),
        check_vma=False,
    )
```

```python
import functools

import jax
import jax.numpy as jnp
from jax import lax
from jax.experimental import pallas as pl
from jax.experimental.pallas import tpu as pltpu
from jax.sharding import PartitionSpec as P

MESH = pl.DeviceIdType.MESH
EXTRA = 128
HALF = 64
CUTS = 2
AHEAD = 2


def order_of(place, n, step):
    both = jnp.minimum(place, n - 1 - place)
    far = (step + 1) // 2
    left = place < n - 1 - place
    near = jnp.where((step % 2 == 1) == left, place - far, place + far)
    rest = jnp.where(left, step, n - 1 - step)
    return jnp.where(step <= 2 * both, near, rest)


def column(row):
    size = row.shape[1]
    spot = lax.broadcasted_iota(jnp.int32, (size, size), 0)
    same = spot == lax.broadcasted_iota(jnp.int32, (size, size), 1)
    picked = jnp.where(same, row.astype(jnp.float32), 0.0)
    return jnp.sum(picked, axis=1, keepdims=True).astype(jnp.int32)


def coefficients(ids, index, table):
    topk, rows = ids.shape
    lane = lax.broadcasted_iota(jnp.int32, (rows, EXTRA), 1)
    entry = lax.broadcasted_iota(jnp.int32, (rows, table.shape[1]), 1)
    named = jnp.zeros((rows, EXTRA), jnp.float32)
    total = jnp.zeros((rows, 1), jnp.float32)
    for k in range(topk):
        weight = jnp.sum(jnp.where(entry == column(index[k : k + 1, :]), table, 0.0), axis=1, keepdims=True)
        named += jnp.where(lane % HALF == column(ids[k : k + 1, :]), weight, 0.0)
        total += weight
    factor = 2.5 * named / total
    high = factor.astype(jnp.bfloat16)
    low = (factor - high.astype(jnp.float32)).astype(jnp.bfloat16)
    return jnp.where(lane < HALF, high.astype(jnp.float32), low.astype(jnp.float32)).astype(jnp.bfloat16)


def kernel(
    n, tok_ref, ids_ref, index_ref, table_ref, wg_hbm, wu_hbm, wd_hbm, out_ref,
    rows_buf, wg, wu, wd, part, core_in, x_out, x_in, z_out, z_right, z_left,
    w_sem, tok_sem,
    zr_send, zl_send, z_recv, xa_send, xa_recv, ca_send, ca_recv, cb_send, cb_recv,
    c_send, c_recv, x_send, x_recv, r_send, r_recv, l_send, l_recv,
):
    me = lax.axis_index("expert")
    sub = lax.axis_index("sub")
    cross, core = sub // 2, sub % 2
    other_core = {"sub": cross * 2 + 1 - core}
    other_x = {"sub": (1 - cross) * 2 + core}
    width = tok_ref.shape[1]
    nr = tok_ref.shape[0]

    copies_w = [
        pltpu.make_async_copy(wg_hbm.at[0], wg, w_sem.at[0]),
        pltpu.make_async_copy(wu_hbm.at[0], wu, w_sem.at[1]),
        pltpu.make_async_copy(wd_hbm.at[0], wd, w_sem.at[2]),
    ]

    def place(c, x):
        return pl.ds(pl.multiple_of((c * 2 + x) * nr, nr), nr)

    mine = place(core, cross)
    copy_tok = pltpu.make_async_copy(tok_ref, rows_buf.at[me, mine, pl.ds(0, width)], tok_sem)
    copy_tok.start()
    for copy in copies_w:
        copy.start()

    barrier = pltpu.get_barrier_semaphore()
    pl.semaphore_signal(barrier, inc=1, device_id=other_core, device_id_type=MESH)
    pl.semaphore_signal(barrier, inc=1, device_id=other_x, device_id_type=MESH)

    @pl.when(me > 0)
    def _():
        pl.semaphore_signal(barrier, inc=1, device_id={"expert": me - 1}, device_id_type=MESH)

    @pl.when(me < n - 1)
    def _():
        pl.semaphore_signal(barrier, inc=1, device_id={"expert": me + 1}, device_id_type=MESH)

    rows_buf[me, mine, pl.ds(width, EXTRA)] = coefficients(
        ids_ref[...], index_ref[...], table_ref[...]
    )
    peers = 2 + jnp.where(me > 0, 1, 0) + jnp.where(me < n - 1, 1, 0)
    pl.semaphore_wait(barrier, peers)
    copy_tok.wait()

    def remote(src, dst, send, recv, device):
        return pltpu.make_async_remote_copy(
            src_ref=src, dst_ref=dst, send_sem=send, recv_sem=recv,
            device_id=device, device_id_type=MESH,
        )

    half = width // CUTS

    def cols(h):
        return pl.ds(h * half, half + (EXTRA if h == CUTS - 1 else 0))

    def cut(h):
        return pl.ds(h * half, half)

    def to_right(b, h):
        ref = rows_buf.at[b, mine, cols(h)]
        return remote(ref, ref, zr_send.at[b, h], z_recv.at[b, h], {"expert": me + 1})

    def to_left(b, h):
        ref = rows_buf.at[b, mine, cols(h)]
        return remote(ref, ref, zl_send.at[b, h], z_recv.at[b, h], {"expert": me - 1})

    def across(b, h):
        ref = rows_buf.at[b, mine, cols(h)]
        return remote(ref, ref, xa_send.at[b, h], xa_recv.at[b, h], other_x)

    def beside(b, h):
        ref = rows_buf.at[b, mine, cols(h)]
        return remote(ref, ref, ca_send.at[b, h], ca_recv.at[b, h], other_core)

    def beside_far(b, h):
        ref = rows_buf.at[b, place(core, 1 - cross), cols(h)]
        return remote(ref, ref, cb_send.at[b, h], cb_recv.at[b, h], other_core)

    def part_beside(b, h):
        return remote(
            part.at[b, pl.ds(pl.multiple_of((1 - core) * 2 * nr, nr), 2 * nr), cut(h)],
            core_in.at[b, :, cut(h)], c_send.at[b, h], c_recv.at[b, h], other_core,
        )

    def part_across(b, h):
        return remote(x_out.at[b, :, cut(h)], x_in.at[b, :, cut(h)], x_send.at[b, h], x_recv.at[b, h], other_x)

    def part_right(b, h):
        return remote(z_out.at[b, :, cut(h)], z_right.at[b, :, cut(h)], r_send.at[b, h], r_recv.at[b, h], {"expert": me + 1})

    def part_left(b, h):
        return remote(z_out.at[b, :, cut(h)], z_left.at[b, :, cut(h)], l_send.at[b, h], l_recv.at[b, h], {"expert": me - 1})

    def spread(b, h):
        @pl.when((b <= me) & (me < n - 1))
        def _():
            to_right(b, h).start()

        @pl.when((b >= me) & (me > 0))
        def _():
            to_left(b, h).start()

        across(b, h).start()
        beside(b, h).start()

    for h in range(CUTS):
        spread(me, h)
    depth = half // 2

    def compute(b):
        gate = jnp.zeros((4 * nr, wg.shape[1]), jnp.float32)
        upper = jnp.zeros((4 * nr, wg.shape[1]), jnp.float32)
        for h in range(CUTS):
            beside(b, h).wait_recv()
            beside_far(b, h).wait_recv()
            for k in range(h * half, (h + 1) * half, depth):
                piece = rows_buf[b, :, k : k + depth]
                gate += jnp.dot(piece, wg[k : k + depth, :], preferred_element_type=jnp.float32)
                upper += jnp.dot(piece, wu[k : k + depth, :], preferred_element_type=jnp.float32)
        extra = rows_buf[b, :, width : width + EXTRA].astype(jnp.float32)
        lane = lax.broadcasted_iota(jnp.int32, extra.shape, 1)
        factor = jnp.sum(jnp.where(lane % HALF == me, extra, 0.0), axis=1, keepdims=True)
        hidden = (gate / (1.0 + jnp.exp(-gate)) * upper * factor).astype(jnp.bfloat16)
        step = half // 4
        for h in range(CUTS):
            for k in range(h * half, (h + 1) * half, step):
                part[b, :, k : k + step] = jnp.dot(
                    hidden, wd[:, k : k + step], preferred_element_type=jnp.float32
                ).astype(jnp.bfloat16)
            part_beside(b, h).start()

    far_rows = pl.ds(pl.multiple_of((1 - cross) * nr, nr), nr)
    own_rows = pl.ds(pl.multiple_of(cross * nr, nr), nr)

    def give_across(b, h):
        part_beside(b, h).wait_recv()
        x_out[b, :, cut(h)] = (
            part[b, place(core, 1 - cross), cut(h)].astype(jnp.float32)
            + core_in[b, far_rows, cut(h)].astype(jnp.float32)
        ).astype(jnp.bfloat16)
        part_across(b, h).start()

    def gather_step(k, carry):
        @pl.when(k < n)
        def _():
            b = order_of(me, n, k)
            for h in range(CUTS):
                to_right(b, h).wait_recv()
                spread(b, h)

        b = order_of(me, n, k - 1)
        for h in range(CUTS):
            across(b, h).wait_recv()
            beside_far(b, h).start()

        @pl.when(k == 1)
        def _():
            for copy in copies_w:
                copy.wait()

        @pl.when(k == n)
        def _():
            for h in range(CUTS):
                give_across(order_of(me, n, n - 2), h)

        compute(b)
        return carry

    lax.fori_loop(1, n + 1, gather_step, 0)

    back = [order_of(me, n, n - 1 - k) for k in range(n)]
    waiting = [(back[k], h) for k in range(n) if k != 1 for h in range(CUTS)]

    def next_across():
        if waiting:
            give_across(*waiting.pop(0))

    for _ in range(AHEAD):
        next_across()

    def reduced(b, h):
        return (
            part[b, mine, cut(h)].astype(jnp.float32)
            + core_in[b, own_rows, cut(h)].astype(jnp.float32)
            + x_in[b, :, cut(h)].astype(jnp.float32)
        )

    for k in (1, 0, *range(2, n - 1)):
        b = back[k]
        for h in range(CUTS):
            part_across(b, h).wait_recv()
            if k != 1:
                next_across()

            @pl.when(b > me)
            def _():
                @pl.when(me > 0)
                def _():
                    part_right(b, h).wait_recv()
                    z_out[b, :, cut(h)] = (
                        reduced(b, h) + z_right[b, :, cut(h)].astype(jnp.float32)
                    ).astype(jnp.bfloat16)

                @pl.when(me == 0)
                def _():
                    z_out[b, :, cut(h)] = reduced(b, h).astype(jnp.bfloat16)

                part_right(b, h).start()

            @pl.when(b < me)
            def _():
                @pl.when(me < n - 1)
                def _():
                    part_left(b, h).wait_recv()
                    z_out[b, :, cut(h)] = (
                        reduced(b, h) + z_left[b, :, cut(h)].astype(jnp.float32)
                    ).astype(jnp.bfloat16)

                @pl.when(me == n - 1)
                def _():
                    z_out[b, :, cut(h)] = reduced(b, h).astype(jnp.bfloat16)

                part_left(b, h).start()

    for h in range(CUTS):
        part_across(me, h).wait_recv()

        @pl.when(me == 0)
        def _():
            part_left(me, h).wait_recv()
            out_ref[:, cut(h)] = (
                reduced(me, h) + z_left[me, :, cut(h)].astype(jnp.float32)
            ).astype(jnp.bfloat16)

        @pl.when(me == n - 1)
        def _():
            part_right(me, h).wait_recv()
            out_ref[:, cut(h)] = (
                reduced(me, h) + z_right[me, :, cut(h)].astype(jnp.float32)
            ).astype(jnp.bfloat16)

        @pl.when((me > 0) & (me < n - 1))
        def _():
            part_right(me, h).wait_recv()
            part_left(me, h).wait_recv()
            out_ref[:, cut(h)] = (
                reduced(me, h)
                + z_left[me, :, cut(h)].astype(jnp.float32)
                + z_right[me, :, cut(h)].astype(jnp.float32)
            ).astype(jnp.bfloat16)

    def finish(b, carry):
        for h in range(CUTS):
            @pl.when((b <= me) & (me < n - 1))
            def _():
                to_right(b, h).wait_send()

            @pl.when((b >= me) & (me > 0))
            def _():
                to_left(b, h).wait_send()

            across(b, h).wait_send()
            beside(b, h).wait_send()
            beside_far(b, h).wait_send()
            part_beside(b, h).wait_send()
            part_across(b, h).wait_send()

            @pl.when(b > me)
            def _():
                part_right(b, h).wait_send()

            @pl.when(b < me)
            def _():
                part_left(b, h).wait_send()

        return carry

    lax.fori_loop(0, n, finish, 0)


def fused(tokens, route_ids, weight_index, combine_table, w_gate, w_up, w_down):
    n = lax.axis_size("expert")
    rows, width = tokens.shape
    units = w_gate.shape[2]
    group = 4 * rows
    bf16 = jnp.bfloat16
    vmem = pl.BlockSpec(memory_space=pltpu.VMEM)
    hbm = pl.BlockSpec(memory_space=pl.ANY)
    dma = pltpu.SemaphoreType.DMA
    block = pltpu.VMEM((n, rows, width), bf16)
    return pl.pallas_call(
        functools.partial(kernel, n),
        out_shape=jax.ShapeDtypeStruct((rows, width), bf16),
        in_specs=[hbm, vmem, vmem, vmem, hbm, hbm, hbm],
        out_specs=vmem,
        scratch_shapes=[
            pltpu.VMEM((n, group, width + EXTRA), bf16),
            pltpu.VMEM((width, units), bf16),
            pltpu.VMEM((width, units), bf16),
            pltpu.VMEM((units, width), bf16),
            pltpu.VMEM((n, group, width), bf16),
            pltpu.VMEM((n, 2 * rows, width), bf16),
            block, block, block, block, block,
            dma((3,)), dma,
        ] + [dma((n, CUTS))] * 17,
        compiler_params=pltpu.CompilerParams(
            collective_id=0, has_side_effects=True, vmem_limit_bytes=56 * 2**20
        ),
    )(tokens, route_ids.T, weight_index.T, combine_table[None, :], w_gate, w_up, w_down)


def fits(tokens, w_gate):
    n, subs = lax.axis_size("expert"), lax.axis_size("sub")
    rows, width = tokens.shape
    held = n * rows * 15 + 3 * w_gate.shape[2]
    return (
        subs == 4 and n == 4 and rows % 16 == 0 and width % 1024 == 0
        and held * width * 2 <= 44 * 2**20
    )


def expert_partial(rows_in, w_gate, w_up, w_down):
    gate = jnp.dot(rows_in, w_gate[0], preferred_element_type=jnp.float32)
    upper = jnp.dot(rows_in, w_up[0], preferred_element_type=jnp.float32)
    hidden = (jax.nn.silu(gate) * upper).astype(jnp.bfloat16)
    return jnp.dot(hidden, w_down[0], preferred_element_type=jnp.float32)


def shards(tokens, route_ids, weight_index, combine_table, w_gate, w_up, w_down):
    if fits(tokens, w_gate):
        return fused(tokens, route_ids, weight_index, combine_table, w_gate, w_up, w_down)
    n_expert = lax.axis_size("expert")
    n_rows, n_width = tokens.shape
    topk = route_ids.shape[1]
    capacity = max(n_rows * topk * 3 // (2 * n_expert), n_rows * topk // n_expert + 2)
    slots_all = n_expert * capacity
    flat_ids = route_ids.reshape(-1)
    onehot = (flat_ids[:, None] == jnp.arange(n_expert, dtype=jnp.int32)[None, :]).astype(jnp.int32)
    earlier = jnp.cumsum(onehot, axis=0) - onehot
    slot = jnp.sum(earlier * onehot, axis=1)
    target = (flat_ids * capacity + slot).reshape(n_rows, topk)
    positions = jnp.arange(slots_all, dtype=jnp.int32)
    select = jnp.any(target[None, :, :] == positions[:, None, None], axis=2)
    send_rows = jnp.dot(
        select.astype(jnp.bfloat16), tokens, preferred_element_type=jnp.float32
    ).astype(jnp.bfloat16)
    landed = lax.all_to_all(send_rows, "expert", split_axis=0, concat_axis=0, tiled=True)
    gathered = lax.all_gather(landed, "sub", axis=0, tiled=True)
    summed = lax.psum_scatter(
        expert_partial(gathered, w_gate, w_up, w_down).astype(jnp.bfloat16),
        "sub",
        scatter_dimension=0,
        tiled=True,
    )
    returned = lax.all_to_all(summed, "expert", split_axis=0, concat_axis=0, tiled=True)
    table_size = combine_table.shape[0]
    weights = jnp.sum(
        jnp.where(
            weight_index[:, :, None] == jnp.arange(table_size, dtype=jnp.int32)[None, None, :],
            combine_table[None, None, :],
            0.0,
        ),
        axis=2,
    )
    mixing = jnp.sum(
        jnp.where(target[:, :, None] == positions[None, None, :], weights[:, :, None], 0.0), axis=1
    )
    total = jnp.dot(mixing, returned.astype(jnp.float32), precision=lax.Precision.HIGHEST)
    return (2.5 * total / jnp.sum(weights, axis=1)[:, None]).astype(jnp.bfloat16)


def solution(mesh):
    return jax.shard_map(
        shards,
        mesh=mesh,
        in_specs=(
            P(("groups", "expert", "sub"), None),
            P(("groups", "expert", "sub"), None),
            P(("groups", "expert", "sub"), None),
            P(),
            P("expert", None, "sub"),
            P("expert", None, "sub"),
            P("expert", "sub", None),
        ),
        out_specs=P(("groups", "expert", "sub"), None),
        check_vma=False,
    )
```

```python
import functools

import jax
import jax.numpy as jnp
from jax import lax
from jax.experimental import pallas as pl
from jax.experimental.pallas import tpu as pltpu
from jax.sharding import PartitionSpec as P

MESH = pl.DeviceIdType.MESH
EXTRA = 128
HALF = 64
CUTS = 2
AHEAD = 2


def order_of(place, n, step):
    both = jnp.minimum(place, n - 1 - place)
    far = (step + 1) // 2
    left = place < n - 1 - place
    near = jnp.where((step % 2 == 1) == left, place - far, place + far)
    rest = jnp.where(left, step, n - 1 - step)
    return jnp.where(step <= 2 * both, near, rest)


def column(row):
    size = row.shape[1]
    spot = lax.broadcasted_iota(jnp.int32, (size, size), 0)
    same = spot == lax.broadcasted_iota(jnp.int32, (size, size), 1)
    picked = jnp.where(same, row.astype(jnp.float32), 0.0)
    return jnp.sum(picked, axis=1, keepdims=True).astype(jnp.int32)


def coefficients(ids, index, table):
    topk, rows = ids.shape
    lane = lax.broadcasted_iota(jnp.int32, (rows, EXTRA), 1)
    entry = lax.broadcasted_iota(jnp.int32, (rows, table.shape[1]), 1)
    named = jnp.zeros((rows, EXTRA), jnp.float32)
    total = jnp.zeros((rows, 1), jnp.float32)
    for k in range(topk):
        weight = jnp.sum(jnp.where(entry == column(index[k : k + 1, :]), table, 0.0), axis=1, keepdims=True)
        named += jnp.where(lane % HALF == column(ids[k : k + 1, :]), weight, 0.0)
        total += weight
    factor = 2.5 * named / total
    high = factor.astype(jnp.bfloat16)
    low = (factor - high.astype(jnp.float32)).astype(jnp.bfloat16)
    return jnp.where(lane < HALF, high.astype(jnp.float32), low.astype(jnp.float32)).astype(jnp.bfloat16)


def kernel(
    n, tok_ref, ids_ref, index_ref, table_ref, wg_hbm, wu_hbm, wd_hbm, out_ref,
    rows_buf, wg, wu, wd, part, core_in, x_out, x_in, z_out, z_right, z_left,
    w_sem, tok_sem,
    zr_send, zl_send, z_recv, xa_send, xa_recv, ca_send, ca_recv, cb_send, cb_recv,
    c_send, c_recv, x_send, x_recv, r_send, r_recv, l_send, l_recv,
):
    me = lax.axis_index("expert")
    sub = lax.axis_index("sub")
    cross, core = sub // 2, sub % 2
    other_core = {"sub": cross * 2 + 1 - core}
    other_x = {"sub": (1 - cross) * 2 + core}
    width = tok_ref.shape[1]
    nr = tok_ref.shape[0]

    copies_w = [
        pltpu.make_async_copy(wg_hbm.at[0], wg, w_sem.at[0]),
        pltpu.make_async_copy(wu_hbm.at[0], wu, w_sem.at[1]),
        pltpu.make_async_copy(wd_hbm.at[0], wd, w_sem.at[2]),
    ]

    def place(c, x):
        return pl.ds(pl.multiple_of((c * 2 + x) * nr, nr), nr)

    mine = place(core, cross)
    copy_tok = pltpu.make_async_copy(tok_ref, rows_buf.at[me, mine, pl.ds(0, width)], tok_sem)
    copy_tok.start()
    for copy in copies_w:
        copy.start()

    barrier = pltpu.get_barrier_semaphore()
    pl.semaphore_signal(barrier, inc=1, device_id=other_core, device_id_type=MESH)
    pl.semaphore_signal(barrier, inc=1, device_id=other_x, device_id_type=MESH)

    @pl.when(me > 0)
    def _():
        pl.semaphore_signal(barrier, inc=1, device_id={"expert": me - 1}, device_id_type=MESH)

    @pl.when(me < n - 1)
    def _():
        pl.semaphore_signal(barrier, inc=1, device_id={"expert": me + 1}, device_id_type=MESH)

    rows_buf[me, mine, pl.ds(width, EXTRA)] = coefficients(
        ids_ref[...], index_ref[...], table_ref[...]
    )
    peers = 2 + jnp.where(me > 0, 1, 0) + jnp.where(me < n - 1, 1, 0)
    pl.semaphore_wait(barrier, peers)
    copy_tok.wait()

    def remote(src, dst, send, recv, device):
        return pltpu.make_async_remote_copy(
            src_ref=src, dst_ref=dst, send_sem=send, recv_sem=recv,
            device_id=device, device_id_type=MESH,
        )

    half = width // CUTS

    def cols(h):
        return pl.ds(h * half, half + (EXTRA if h == CUTS - 1 else 0))

    def cut(h):
        return pl.ds(h * half, half)

    def to_right(b, h):
        ref = rows_buf.at[b, mine, cols(h)]
        return remote(ref, ref, zr_send.at[b, h], z_recv.at[b, h], {"expert": me + 1})

    def to_left(b, h):
        ref = rows_buf.at[b, mine, cols(h)]
        return remote(ref, ref, zl_send.at[b, h], z_recv.at[b, h], {"expert": me - 1})

    def across(b, h):
        ref = rows_buf.at[b, mine, cols(h)]
        return remote(ref, ref, xa_send.at[b, h], xa_recv.at[b, h], other_x)

    def beside(b, h):
        ref = rows_buf.at[b, mine, cols(h)]
        return remote(ref, ref, ca_send.at[b, h], ca_recv.at[b, h], other_core)

    def beside_far(b, h):
        ref = rows_buf.at[b, place(core, 1 - cross), cols(h)]
        return remote(ref, ref, cb_send.at[b, h], cb_recv.at[b, h], other_core)

    def part_beside(b, h):
        return remote(
            part.at[b, pl.ds(pl.multiple_of((1 - core) * 2 * nr, nr), 2 * nr), cut(h)],
            core_in.at[b, :, cut(h)], c_send.at[b, h], c_recv.at[b, h], other_core,
        )

    def part_across(b, h):
        return remote(x_out.at[b, :, cut(h)], x_in.at[b, :, cut(h)], x_send.at[b, h], x_recv.at[b, h], other_x)

    def part_right(b, h):
        return remote(z_out.at[b, :, cut(h)], z_right.at[b, :, cut(h)], r_send.at[b, h], r_recv.at[b, h], {"expert": me + 1})

    def part_left(b, h):
        return remote(z_out.at[b, :, cut(h)], z_left.at[b, :, cut(h)], l_send.at[b, h], l_recv.at[b, h], {"expert": me - 1})

    def spread(b, h):
        @pl.when((b <= me) & (me < n - 1))
        def _():
            to_right(b, h).start()

        @pl.when((b >= me) & (me > 0))
        def _():
            to_left(b, h).start()

        across(b, h).start()
        beside(b, h).start()

    for h in range(CUTS):
        spread(me, h)
    depth = 1024

    def compute(b):
        gate = jnp.zeros((4 * nr, wg.shape[1]), jnp.float32)
        upper = jnp.zeros((4 * nr, wg.shape[1]), jnp.float32)
        for k in range(0, width, depth):
            piece = rows_buf[b, :, k : k + depth]
            gate += jnp.dot(piece, wg[k : k + depth, :], preferred_element_type=jnp.float32)
            upper += jnp.dot(piece, wu[k : k + depth, :], preferred_element_type=jnp.float32)
        extra = rows_buf[b, :, width : width + EXTRA].astype(jnp.float32)
        lane = lax.broadcasted_iota(jnp.int32, extra.shape, 1)
        factor = jnp.sum(jnp.where(lane % HALF == me, extra, 0.0), axis=1, keepdims=True)
        hidden = (gate / (1.0 + jnp.exp(-gate)) * upper * factor).astype(jnp.bfloat16)
        step = half // 4
        for h in range(CUTS):
            for k in range(h * half, (h + 1) * half, step):
                part[b, :, k : k + step] = jnp.dot(
                    hidden, wd[:, k : k + step], preferred_element_type=jnp.float32
                ).astype(jnp.bfloat16)
            part_beside(b, h).start()

    far_rows = pl.ds(pl.multiple_of((1 - cross) * nr, nr), nr)
    own_rows = pl.ds(pl.multiple_of(cross * nr, nr), nr)

    def give_across(b, h):
        part_beside(b, h).wait_recv()
        x_out[b, :, cut(h)] = (
            part[b, place(core, 1 - cross), cut(h)].astype(jnp.float32)
            + core_in[b, far_rows, cut(h)].astype(jnp.float32)
        ).astype(jnp.bfloat16)
        part_across(b, h).start()

    def gather_step(k, carry):
        @pl.when(k < n)
        def _():
            b = order_of(me, n, k)
            for h in range(CUTS):
                to_right(b, h).wait_recv()
                spread(b, h)

        b = order_of(me, n, k - 1)
        for h in range(CUTS):
            across(b, h).wait_recv()
            beside_far(b, h).start()

        @pl.when(k == 1)
        def _():
            for copy in copies_w:
                copy.wait()

        @pl.when(k == n)
        def _():
            for h in range(CUTS):
                give_across(order_of(me, n, n - 2), h)

        for h in range(CUTS):
            beside(b, h).wait_recv()
            beside_far(b, h).wait_recv()
        compute(b)
        return carry

    lax.fori_loop(1, n + 1, gather_step, 0)

    back = [order_of(me, n, n - 1 - k) for k in range(n)]
    waiting = [(back[k], h) for k in range(n) if k != 1 for h in range(CUTS)]

    def next_across():
        if waiting:
            give_across(*waiting.pop(0))

    for _ in range(AHEAD):
        next_across()

    def reduced(b, h):
        return (
            part[b, mine, cut(h)].astype(jnp.float32)
            + core_in[b, own_rows, cut(h)].astype(jnp.float32)
            + x_in[b, :, cut(h)].astype(jnp.float32)
        )

    for k in (1, 0, *range(2, n - 1)):
        b = back[k]
        for h in range(CUTS):
            part_across(b, h).wait_recv()
            if k != 1:
                next_across()

            @pl.when(b > me)
            def _():
                @pl.when(me > 0)
                def _():
                    part_right(b, h).wait_recv()
                    z_out[b, :, cut(h)] = (
                        reduced(b, h) + z_right[b, :, cut(h)].astype(jnp.float32)
                    ).astype(jnp.bfloat16)

                @pl.when(me == 0)
                def _():
                    z_out[b, :, cut(h)] = reduced(b, h).astype(jnp.bfloat16)

                part_right(b, h).start()

            @pl.when(b < me)
            def _():
                @pl.when(me < n - 1)
                def _():
                    part_left(b, h).wait_recv()
                    z_out[b, :, cut(h)] = (
                        reduced(b, h) + z_left[b, :, cut(h)].astype(jnp.float32)
                    ).astype(jnp.bfloat16)

                @pl.when(me == n - 1)
                def _():
                    z_out[b, :, cut(h)] = reduced(b, h).astype(jnp.bfloat16)

                part_left(b, h).start()

    for h in range(CUTS):
        part_across(me, h).wait_recv()

        @pl.when(me == 0)
        def _():
            part_left(me, h).wait_recv()
            out_ref[:, cut(h)] = (
                reduced(me, h) + z_left[me, :, cut(h)].astype(jnp.float32)
            )

        @pl.when(me == n - 1)
        def _():
            part_right(me, h).wait_recv()
            out_ref[:, cut(h)] = (
                reduced(me, h) + z_right[me, :, cut(h)].astype(jnp.float32)
            )

        @pl.when((me > 0) & (me < n - 1))
        def _():
            part_right(me, h).wait_recv()
            part_left(me, h).wait_recv()
            out_ref[:, cut(h)] = (
                reduced(me, h)
                + z_left[me, :, cut(h)].astype(jnp.float32)
                + z_right[me, :, cut(h)].astype(jnp.float32)
            )

    def finish(b, carry):
        for h in range(CUTS):
            @pl.when((b <= me) & (me < n - 1))
            def _():
                to_right(b, h).wait_send()

            @pl.when((b >= me) & (me > 0))
            def _():
                to_left(b, h).wait_send()

            across(b, h).wait_send()
            beside(b, h).wait_send()
            beside_far(b, h).wait_send()
            part_beside(b, h).wait_send()
            part_across(b, h).wait_send()

            @pl.when(b > me)
            def _():
                part_right(b, h).wait_send()

            @pl.when(b < me)
            def _():
                part_left(b, h).wait_send()

        return carry

    lax.fori_loop(0, n, finish, 0)


def fused(tokens, route_ids, weight_index, combine_table, w_gate, w_up, w_down):
    n = lax.axis_size("expert")
    rows, width = tokens.shape
    units = w_gate.shape[2]
    group = 4 * rows
    bf16 = jnp.bfloat16
    vmem = pl.BlockSpec(memory_space=pltpu.VMEM)
    hbm = pl.BlockSpec(memory_space=pl.ANY)
    dma = pltpu.SemaphoreType.DMA
    block = pltpu.VMEM((n, rows, width), bf16)
    return pl.pallas_call(
        functools.partial(kernel, n),
        out_shape=jax.ShapeDtypeStruct((rows, width), jnp.float32),
        in_specs=[hbm, vmem, vmem, vmem, hbm, hbm, hbm],
        out_specs=vmem,
        scratch_shapes=[
            pltpu.VMEM((n, group, width + EXTRA), bf16),
            pltpu.VMEM((width, units), bf16),
            pltpu.VMEM((width, units), bf16),
            pltpu.VMEM((units, width), bf16),
            pltpu.VMEM((n, group, width), bf16),
            pltpu.VMEM((n, 2 * rows, width), bf16),
            block, block, block, block, block,
            dma((3,)), dma,
        ] + [dma((n, CUTS))] * 17,
        compiler_params=pltpu.CompilerParams(
            collective_id=0, has_side_effects=True, vmem_limit_bytes=56 * 2**20
        ),
    )(tokens, route_ids.T, weight_index.T, combine_table[None, :], w_gate, w_up, w_down).astype(bf16)


def fits(tokens, w_gate):
    n, subs = lax.axis_size("expert"), lax.axis_size("sub")
    rows, width = tokens.shape
    held = n * rows * 15 + 3 * w_gate.shape[2]
    return (
        subs == 4 and n == 4 and rows % 16 == 0 and width % 1024 == 0
        and held * width * 2 <= 44 * 2**20
    )


def expert_partial(rows_in, w_gate, w_up, w_down):
    gate = jnp.dot(rows_in, w_gate[0], preferred_element_type=jnp.float32)
    upper = jnp.dot(rows_in, w_up[0], preferred_element_type=jnp.float32)
    hidden = (jax.nn.silu(gate) * upper).astype(jnp.bfloat16)
    return jnp.dot(hidden, w_down[0], preferred_element_type=jnp.float32)


def shards(tokens, route_ids, weight_index, combine_table, w_gate, w_up, w_down):
    if fits(tokens, w_gate):
        return fused(tokens, route_ids, weight_index, combine_table, w_gate, w_up, w_down)
    n_expert = lax.axis_size("expert")
    n_rows, n_width = tokens.shape
    topk = route_ids.shape[1]
    capacity = max(n_rows * topk * 3 // (2 * n_expert), n_rows * topk // n_expert + 2)
    slots_all = n_expert * capacity
    flat_ids = route_ids.reshape(-1)
    onehot = (flat_ids[:, None] == jnp.arange(n_expert, dtype=jnp.int32)[None, :]).astype(jnp.int32)
    earlier = jnp.cumsum(onehot, axis=0) - onehot
    slot = jnp.sum(earlier * onehot, axis=1)
    target = (flat_ids * capacity + slot).reshape(n_rows, topk)
    positions = jnp.arange(slots_all, dtype=jnp.int32)
    select = jnp.any(target[None, :, :] == positions[:, None, None], axis=2)
    send_rows = jnp.dot(
        select.astype(jnp.bfloat16), tokens, preferred_element_type=jnp.float32
    ).astype(jnp.bfloat16)
    landed = lax.all_to_all(send_rows, "expert", split_axis=0, concat_axis=0, tiled=True)
    gathered = lax.all_gather(landed, "sub", axis=0, tiled=True)
    summed = lax.psum_scatter(
        expert_partial(gathered, w_gate, w_up, w_down).astype(jnp.bfloat16),
        "sub",
        scatter_dimension=0,
        tiled=True,
    )
    returned = lax.all_to_all(summed, "expert", split_axis=0, concat_axis=0, tiled=True)
    table_size = combine_table.shape[0]
    weights = jnp.sum(
        jnp.where(
            weight_index[:, :, None] == jnp.arange(table_size, dtype=jnp.int32)[None, None, :],
            combine_table[None, None, :],
            0.0,
        ),
        axis=2,
    )
    mixing = jnp.sum(
        jnp.where(target[:, :, None] == positions[None, None, :], weights[:, :, None], 0.0), axis=1
    )
    total = jnp.dot(mixing, returned.astype(jnp.float32), precision=lax.Precision.HIGHEST)
    return (2.5 * total / jnp.sum(weights, axis=1)[:, None]).astype(jnp.bfloat16)


def solution(mesh):
    return jax.shard_map(
        shards,
        mesh=mesh,
        in_specs=(
            P(("groups", "expert", "sub"), None),
            P(("groups", "expert", "sub"), None),
            P(("groups", "expert", "sub"), None),
            P(),
            P("expert", None, "sub"),
            P("expert", None, "sub"),
            P("expert", "sub", None),
        ),
        out_specs=P(("groups", "expert", "sub"), None),
        check_vma=False,
    )
```
